256 devices in a mesh: sweep: 8 (over y, core), leaf: 32 (over z, x).
Axes of the slice: x: 4, y: 4, z: 8, core: 2. Of those that a mesh axis runs over, the one named last changes fastest.
Arguments:
- rhs: bfloat16 [8, 256, 32, 512], P('sweep', 'leaf'), may hold values from -6 to 6
- incoming: bfloat16 [256, 32, 512], P('leaf'), may hold values from -6 to 6
- front_inv: bfloat16 [8, 256, 2, 256, 256], P('sweep', 'leaf'), may hold values from -0.21875 to 0.21875
- coupling: bfloat16 [8, 256, 2, 256, 256], P('sweep', 'leaf'), may hold values from -0.25 to 0.25
- update: bfloat16 [8, 256, 4, 2, 256, 256], P('sweep', 'leaf'), may hold values from -0.09375 to 0.09375
- dest_owner: int32 [256, 4], P('leaf'), may hold values from 0 to 31, all different within a row; in each aligned block of 8 rows (0 to 7, 8 to 15, ...) at most 2 rows name the same one
- dest_front: int32 [256, 4], P('leaf'), may hold values from 0 to 7
Outputs:
- solution: bfloat16 [8, 256, 32, 512], P('sweep', 'leaf')
The draws below stay inside these ranges and needn't reach their ends.
Inputs may be any that keep to these rules, and one draw needn't show every extreme that they name: `dest_owner`: among the rows of one index of leaf no owner is named more than 2 times, and that bound is reached; a front names 4 different owners.
All inputs are finite; a program needn't handle non-finite values.
Results may differ from the reference program's by a relative error of at most 0.03.
Values may be sent and summed in bfloat16 or wider, within the bound.
A program may use at most 128 MiB of HBM per device.

```python
import math
import jax
import jax.numpy as jnp
import numpy as np

F = 256
NRHS = 32
FR_DEV = 8
K = 4
MOST = 2
PANELS = 8
FRONTS = 256
N_LEAF = 32


def touch_ends(result, stream_key, smallest, high):
    index_at = [jax.random.randint(jax.random.fold_in(stream_key, axis), (), 0, length) for axis, length in enumerate(result.shape)]
    widest = result.shape.index(max(result.shape))
    beside = index_at[:widest] + [(index_at[widest] + 1) % result.shape[widest]] + index_at[widest + 1:]
    return result.at[tuple(index_at)].set(smallest).at[tuple(beside)].set(high)


def shard_levels(stream_key, shape, split, low, high):
    def one(dim, parts):
        steps = jax.random.uniform(jax.random.fold_in(jax.random.fold_in(stream_key, 6), dim), (parts,), jnp.float32, low / len(split), high / len(split))
        return jnp.repeat(jnp.exp(steps), shape[dim] // parts).reshape((-1,) + (1,) * (len(shape) - dim - 1))

    level = one(*split[0])
    for cut in split[1:]:
        level = level * one(*cut)
    return level


def routed_block(own_key, own, number, rows, number_of, top, reach, skew):
    order = jax.random.permutation(own_key, number_of)
    heavy_load, common = shares(number_of, rows * top, reach, skew, True), shares(number_of, rows * top, reach, skew, False)
    places = jnp.arange(number_of)

    def named(tallies, offset_by):
        used = int((tallies > 0).sum())
        fixed = max(1, used // 4)
        passed = fixed + (places - fixed + offset_by * (used - fixed)) % max(1, number_of - fixed)
        return jnp.zeros((number_of,), jnp.int32).at[order[jnp.where(places < fixed, places, passed)]].set(jnp.asarray(tallies, jnp.int32))

    tallies = jnp.where(number % 4 == 0, named(heavy_load, number // 4), named(common, number - number // 4 - 1))
    mixed = jax.random.permutation(jax.random.fold_in(own, 3), number_of)
    source_of, sink = mixed[0:number_of // 2 * 2:2], mixed[1:number_of // 2 * 2:2]
    slack = jnp.minimum(tallies[source_of] - 1, reach - tallies[sink]) // 2
    slack = jnp.where((source_of == order[0]) | (sink == order[0]) | (tallies[sink] == 0), 0, jnp.maximum(slack, 0))
    passed = jax.random.randint(jax.random.fold_in(own, 4), (number_of // 2,), 0, 1 << 20) % (slack + 1)
    tallies = tallies.at[source_of].add(-passed).at[sink].add(passed)
    items = jnp.searchsorted(jnp.cumsum(tallies), jnp.arange(rows * top), side="right").astype(jnp.int32)
    table = items.reshape(top, rows).T
    table = table[jax.random.permutation(jax.random.fold_in(own, 1), rows)]
    offset_by = jax.random.randint(jax.random.fold_in(own, 2), (rows, 1), 0, top)
    return jnp.take_along_axis(table, (jnp.arange(top)[None, :] + offset_by) % top, axis=1)


def shares(count, total, most, lean, full):
    weights = [(1 << 20) // math.isqrt(standing ** lean) + 1 for standing in range(1, count + 1)]
    largest = most if full else min(most, max(-(-total // count), total * weights[0] // sum(weights)))
    least = 1 if total - largest >= count - 1 else 0
    holding, spare = [largest] + [least] * (count - 1), total - largest - least * (count - 1)
    while spare > 0:
        free = [i for i in range(1, count) if holding[i] < largest] or [i for i in range(1, count) if holding[i] < most]
        mass, left = sum([weights[i] for i in free]), spare
        for i in free:
            more = min(most - holding[i], max(1, left * weights[i] // mass), spare)
            holding[i] = holding[i] + more
            spare = spare - more
    return np.array(holding)


def gaussian(own_key, dims, scale, limit, cuts=(), dtype=jnp.bfloat16):
    entries = scale * jax.random.normal(own_key, dims, jnp.float32)
    if cuts:
        entries = entries * shard_levels(own_key, dims, cuts, -0.22, 0.18)
    return jnp.clip(entries, -limit, limit).astype(dtype)


def setup_inputs(seed: int = 0) -> dict:
    key_list = jax.random.split(jax.random.key(seed), 8)
    rhs = gaussian(key_list[0], (PANELS, FRONTS, NRHS, 2 * F), 1.0, 6.0, ((0, 8), (1, 32)))
    incoming = gaussian(key_list[1], (FRONTS, NRHS, 2 * F), 1.0, 6.0, ((0, 32),))
    front_inv = gaussian(key_list[2], (PANELS, FRONTS, 2, F, F), (3 * F) ** -0.5, 0.21875, ((0, 8), (1, 32)))
    coupling = gaussian(key_list[3], (PANELS, FRONTS, 2, F, F), (2 * F) ** -0.5, 0.25, ((0, 8), (1, 32)))
    update = gaussian(key_list[4], (PANELS, FRONTS, K, 2, F, F), (4 * F * K) ** -0.5, 0.09375, ((0, 8), (1, 32)))
    dest_owner_keys = jax.random.split(jax.random.fold_in(key_list[5], 1), FRONTS // FR_DEV)
    dest_owner_turns = jax.random.permutation(jax.random.fold_in(key_list[5], 3), FRONTS // FR_DEV)
    dest_owner = jax.vmap(lambda own, number: routed_block(jax.random.fold_in(key_list[5], 2), own, number, FR_DEV, N_LEAF, K, MOST, 2))(dest_owner_keys, dest_owner_turns).reshape((FRONTS, K))
    dest_front = touch_ends(jax.random.randint(key_list[6], (FRONTS, K), 0, FR_DEV), jax.random.fold_in(key_list[6], 1), 0, FR_DEV - 1).astype(jnp.int32)
    return {"rhs": rhs, "incoming": incoming, "front_inv": front_inv, "coupling": coupling, "update": update, "dest_owner": dest_owner, "dest_front": dest_front}


def complex_apply(vectors, matrix):
    width = matrix.shape[-1]
    real_in = vectors[..., :width].astype(jnp.float32)
    imag_in = vectors[..., width:].astype(jnp.float32)
    real_mat = matrix[..., 0, :, :].astype(jnp.float32)
    imag_mat = matrix[..., 1, :, :].astype(jnp.float32)
    real_out = jnp.matmul(real_in, real_mat) - jnp.matmul(imag_in, imag_mat)
    imag_out = jnp.matmul(real_in, imag_mat) + jnp.matmul(imag_in, real_mat)
    return jnp.concatenate([real_out, imag_out], axis=-1)


def reference(rhs, incoming, front_inv, coupling, update, dest_owner, dest_front):
    target = (dest_owner * FR_DEV + dest_front).reshape(-1).astype(jnp.int32)
    previous = incoming
    results = []
    for panel in range(PANELS):
        field = rhs[panel].astype(jnp.float32) - complex_apply(previous, coupling[panel])
        field_half = field.astype(jnp.bfloat16)
        first = complex_apply(field_half, front_inv[panel]).astype(jnp.bfloat16)
        contribution = complex_apply(first[:, None], update[panel]).astype(jnp.bfloat16)
        flat = contribution.reshape(FRONTS * K, NRHS, 2 * F).astype(jnp.float32)
        arrived = jnp.zeros((FRONTS, NRHS, 2 * F), jnp.float32).at[target].add(flat)
        remainder = (field - arrived).astype(jnp.bfloat16)
        solved = complex_apply(remainder, front_inv[panel]).astype(jnp.bfloat16)
        results.append(solved)
        previous = solved
    return jnp.stack(results)
```

```python
import functools

import jax
import jax.numpy as jnp
from jax import lax
from jax.experimental import pallas as pl
from jax.experimental.pallas import tpu as pltpu
from jax.sharding import PartitionSpec as P

ROWS = 4
SLOTS = 2
SKEW = 1
MESH = pl.DeviceIdType.MESH
F32 = jnp.float32
BF16 = jnp.bfloat16


def dot(a, b):
    return jnp.dot(a, b, preferred_element_type=F32)


def turned(x, rows):
    count, width = x.shape
    both = 2 * rows
    value = x.reshape(count // both, both, width)
    value = pltpu.roll(value, rows, 1)
    row = lax.broadcasted_iota(jnp.int32, value.shape, 1)
    return jnp.where(row < rows, -value, value).reshape(count, width)


def kernel(
    leafs, sweeps, rhs_ref, inc_ref, finv_hbm, coup_hbm, upd_hbm, own_ref, front_ref, out_ref,
    finv, coup, upd, comp, place, take, rhs_s, rhs_u, sol_s, contrib, field, prev, done, sent, got, told, heard,
    load_sem, prev_send, prev_recv, send_sem, recv_sem, tell_send, tell_recv,
):
    fronts, total_rows, doubled = rhs_ref.shape[1:]
    width = doubled // 2
    blocks = own_ref.shape[1]
    groups = total_rows // ROWS
    both = 2 * ROWS
    per = SLOTS * both
    pairs = fronts * blocks
    me = lax.axis_index("leaf")
    level = lax.axis_index("sweep")

    loads = [
        pltpu.make_async_copy(coup_hbm, coup, load_sem.at[0]),
        pltpu.make_async_copy(finv_hbm, finv, load_sem.at[1]),
        pltpu.make_async_copy(upd_hbm, upd, load_sem.at[2]),
    ]
    for load in loads:
        load.start()

    barrier = pltpu.get_barrier_semaphore()
    for off in range(1, leafs):
        pl.semaphore_signal(barrier, inc=1, device_id=(level, lax.rem(me + off, leafs)), device_id_type=MESH)

    @pl.when(level > 0)
    def _():
        pl.semaphore_signal(barrier, inc=1, device_id=(level - 1, me), device_id_type=MESH)

    @pl.when(level < sweeps - 1)
    def _():
        pl.semaphore_signal(barrier, inc=1, device_id=(level + 1, me), device_id_type=MESH)

    above = jnp.where(level > 0, 1, 0)
    below = jnp.where(level < sweeps - 1, 1, 0)
    pl.semaphore_wait(barrier, leafs - 1 + above + below)

    lane = lax.broadcasted_iota(jnp.int32, (fronts, pairs * both), 1)
    sub = lax.broadcasted_iota(jnp.int32, (fronts, pairs * both), 0)
    lane_front = lane // (blocks * both)
    lane_block = (lane // both) % blocks
    own = own_ref[...]
    front = front_ref[...]
    own_l = jnp.zeros_like(lane)
    front_l = jnp.zeros_like(lane)
    for k in range(blocks):
        here = (lane_block == k) & (lane_front == sub)
        own_l += jnp.where(here, own[:, k : k + 1], 0)
        front_l += jnp.where(here, front[:, k : k + 1] + 1, 0)
    own_l = jnp.sum(own_l, axis=0, keepdims=True)
    front_l = jnp.sum(front_l, axis=0, keepdims=True)
    rank = jnp.zeros_like(lane)
    for k in range(blocks):
        rank += jnp.where((own[:, k : k + 1] == own_l) & (sub < lane_front), 1, 0)
    rank = jnp.sum(rank, axis=0, keepdims=True)
    goal = (own_l * SLOTS + rank) * both + lane[:1] % both
    row = lax.broadcasted_iota(jnp.int32, (leafs * per, pairs * both), 0)
    hot = row == goal
    place[...] = jnp.where(hot, 1.0, 0.0).astype(BF16)
    labels = jnp.where(hot, front_l.astype(F32), 0.0).astype(BF16)
    told[...] = dot(labels, jnp.ones((pairs * both, 128), BF16)).astype(BF16)

    def spread(source, target, sends, recvs):
        for off in range(1, leafs):
            to = lax.rem(me + off, leafs)
            pltpu.make_async_remote_copy(
                src_ref=source.at[pl.ds(pl.multiple_of(to * per, per), per)],
                dst_ref=target.at[pl.ds(pl.multiple_of(me * per, per), per)],
                send_sem=sends,
                recv_sem=recvs,
                device_id=(level, to),
                device_id_type=MESH,
            ).start()
        mine = pl.ds(pl.multiple_of(me * per, per), per)
        target[mine, :] = source[mine, :]

    def wait_spread(ref, sem):
        part = ref.at[pl.ds(0, (leafs - 1) * per)]
        pltpu.make_async_copy(part, part, sem).wait()

    spread(told, heard, tell_send, tell_recv)

    g_row = lax.broadcasted_iota(jnp.int32, (groups * both, 2 * total_rows), 0)
    g_col = lax.broadcasted_iota(jnp.int32, (groups * both, 2 * total_rows), 1)
    from_row = ((g_row // ROWS) % 2) * total_rows + (g_row // both) * ROWS + g_row % ROWS
    regroup = jnp.where(g_col == from_row, 1.0, 0.0).astype(BF16)

    def grouped(value):
        return dot(regroup, jnp.concatenate([value[:, :width], value[:, width:]], axis=0))

    @pl.when(level == 0)
    def _():
        values = [grouped(inc_ref[i]) for i in range(fronts)]
        for g in range(groups):
            parts = [value[g * both : (g + 1) * both] for value in values]
            prev[g] = jnp.concatenate(parts, axis=0).astype(BF16)

    for load in loads:
        load.wait()

    def stacked(x):
        return jnp.concatenate([x, turned(x, ROWS)], axis=1).astype(BF16)

    def prepare(i, carry):
        value = grouped(rhs_ref[0, i])
        at_i = pl.ds(pl.multiple_of(i * both, both), both)
        for g in range(groups):
            rhs_s[g, at_i, :] = value[g * both : (g + 1) * both]
        a = finv[i].reshape(2 * width, width)
        first = stacked(dot(stacked(value), a))
        c = coup[i].reshape(2 * width, width)
        c_turned = jnp.concatenate([-c[width:], c[:width]], axis=0)
        ca = dot(jnp.concatenate([c, c_turned], axis=1), a)
        ca = ca.astype(BF16)
        ca = jnp.concatenate([ca, jnp.concatenate([-ca[width:], ca[:width]], axis=0)], axis=1)
        for k in range(blocks):
            u = upd[i, k].reshape(2 * width, width)
            comp[i, k] = dot(ca, u).astype(BF16)
            part = dot(first, u)
            at_ik = pl.ds(pl.multiple_of((i * blocks + k) * both, both), both)
            for g in range(groups):
                rhs_u[g, at_ik, :] = part[g * both : (g + 1) * both]
        return carry

    lax.fori_loop(0, fronts, prepare, 0)

    wait_spread(heard, tell_recv)
    h = heard[...].astype(F32)
    t_row = lax.broadcasted_iota(jnp.int32, h.shape, 0)
    t_lane = lax.broadcasted_iota(jnp.int32, h.shape, 1)
    fits = (h == (t_lane // both + 1).astype(F32)) & (t_row % both == t_lane % both)
    take[...] = jnp.where(fits, 1.0, 0.0).T.astype(BF16)[: fronts * both]

    def begin(g):
        @pl.when(level > 0)
        def _():
            pltpu.make_async_copy(prev.at[g], prev.at[g], prev_recv.at[g]).wait()

        x = stacked(prev[g].astype(F32))
        for i in range(fronts):
            x_i = x[i * both : (i + 1) * both]
            for k in range(blocks):
                at = (i * blocks + k) * both
                contrib[at : at + both, :] = rhs_u[g, at : at + both, :] - dot(x_i, comp[i, k])
        sent[g] = dot(place[...], contrib[...].astype(BF16)).astype(BF16)
        spread(sent.at[g], got.at[g], send_sem.at[g], recv_sem.at[g])
        for i in range(fronts):
            x_i = x[i * both : (i + 1) * both]
            at = i * both
            field[g, at : at + both, :] = rhs_s[g, at : at + both, :] - dot(x_i, coup[i].reshape(2 * width, width))

    def pass_down(g):
        return pltpu.make_async_remote_copy(
            src_ref=done.at[g],
            dst_ref=prev.at[g],
            send_sem=prev_send.at[g],
            recv_sem=prev_recv.at[g],
            device_id=(level + 1, me),
            device_id_type=MESH,
        )

    def finish(g):
        wait_spread(got.at[g], recv_sem.at[g])
        rest = field[g] - dot(take[...], got[g])
        y = stacked(rest.astype(BF16).astype(F32))
        at_g = pl.ds(pl.multiple_of(g * both, both), both)
        values = []
        for i in range(fronts):
            value = dot(y[i * both : (i + 1) * both], finv[i].reshape(2 * width, width))
            sol_s[i, at_g, :] = value
            values.append(value)
        done[g] = jnp.concatenate(values, axis=0).astype(BF16)

        @pl.when(level < sweeps - 1)
        def _():
            pass_down(g).start()

    def advance(g, carry):
        begin(g)

        @pl.when(g >= SKEW)
        def _():
            finish(g - SKEW)

        return carry

    lax.fori_loop(0, groups, advance, 0)
    for g in range(groups - SKEW, groups):
        finish(g)

    o_row = lax.broadcasted_iota(jnp.int32, (2 * total_rows, groups * both), 0)
    o_col = lax.broadcasted_iota(jnp.int32, (2 * total_rows, groups * both), 1)
    to_row = ((o_col // ROWS) % 2) * total_rows + (o_col // both) * ROWS + o_col % ROWS
    ungroup = jnp.where(o_row == to_row, 1.0, 0.0).astype(BF16)
    for i in range(fronts):
        value = dot(ungroup, sol_s[i].astype(BF16)).astype(BF16)
        out_ref[0, i, :, :width] = value[:total_rows]
        out_ref[0, i, :, width:] = value[total_rows:]

    def drain(g, carry):
        wait_spread(sent.at[g], send_sem.at[g])

        @pl.when(level < sweeps - 1)
        def _():
            pass_down(g).wait_send()

        return carry

    lax.fori_loop(0, groups, drain, 0)
    wait_spread(told, tell_send)


def body(leafs, sweeps, rhs, incoming, front_inv, coupling, update, dest_owner, dest_front):
    fronts, total_rows, doubled = incoming.shape
    width = doubled // 2
    blocks = dest_owner.shape[1]
    groups = total_rows // ROWS
    both = 2 * ROWS
    slots = leafs * SLOTS * both
    pairs = fronts * blocks
    vmem = pl.BlockSpec(memory_space=pltpu.VMEM)
    hbm = pl.BlockSpec(memory_space=pl.ANY)
    dma = pltpu.SemaphoreType.DMA
    return pl.pallas_call(
        functools.partial(kernel, leafs, sweeps),
        out_shape=jax.ShapeDtypeStruct(rhs.shape, BF16),
        in_specs=[vmem, vmem, hbm, hbm, hbm, vmem, vmem],
        out_specs=vmem,
        scratch_shapes=[
            pltpu.VMEM(front_inv.shape[1:], BF16),
            pltpu.VMEM(coupling.shape[1:], BF16),
            pltpu.VMEM(update.shape[1:], BF16),
            pltpu.VMEM((fronts, blocks, 2 * width, width), BF16),
            pltpu.VMEM((slots, pairs * both), BF16),
            pltpu.VMEM((fronts * both, slots), BF16),
            pltpu.VMEM((groups, fronts * both, width), F32),
            pltpu.VMEM((groups, pairs * both, width), F32),
            pltpu.VMEM((fronts, groups * both, width), F32),
            pltpu.VMEM((pairs * both, width), F32),
            pltpu.VMEM((groups, fronts * both, width), F32),
            pltpu.VMEM((groups, fronts * both, width), BF16),
            pltpu.VMEM((groups, fronts * both, width), BF16),
            pltpu.VMEM((groups, slots, width), BF16),
            pltpu.VMEM((groups, slots, width), BF16),
            pltpu.VMEM((slots, 128), BF16),
            pltpu.VMEM((slots, 128), BF16),
            dma((3,)),
            dma((groups,)),
            dma((groups,)),
            dma((groups,)),
            dma((groups,)),
            dma,
            dma,
        ],
        compiler_params=pltpu.CompilerParams(
            collective_id=0, has_side_effects=True, vmem_limit_bytes=60 * 1024 * 1024
        ),
    )(rhs, incoming, front_inv[0], coupling[0], update[0], dest_owner, dest_front)


def solution(mesh):
    return jax.shard_map(
        functools.partial(body, mesh.shape["leaf"], mesh.shape["sweep"]),
        mesh=mesh,
        in_specs=(
            P("sweep", "leaf", None, None),
            P("leaf", None, None),
            P("sweep", "leaf", None, None, None),
            P("sweep", "leaf", None, None, None),
            P("sweep", "leaf", None, None, None, None),
            P("leaf", None),
            P("leaf", None),
        ),
        out_specs=P("sweep", "leaf", None, None),
        check_vma=False,
    )
```

```python
import functools

import jax
import jax.numpy as jnp
from jax import lax
from jax.experimental import pallas as pl
from jax.experimental.pallas import tpu as pltpu
from jax.sharding import PartitionSpec as P

ROWS = 2
SLOTS = 2
LANES = 128
TOGETHER = 2
LEAF_X = 4
UNIT = 8
PER = SLOTS * UNIT
SKEW = 3
MESH = pl.DeviceIdType.MESH
F32 = jnp.float32
BF16 = jnp.bfloat16


def dot(a, b):
    return jnp.dot(a, b, preferred_element_type=F32)


def expand(v):
    a = v.reshape(v.shape[0] // UNIT, UNIT, LANES)
    b = pltpu.roll(a, UNIT // 2, 1)
    row = lax.broadcasted_iota(jnp.int32, a.shape, 1)
    first = jnp.where(row < UNIT // 2, a, b)
    second = jnp.where(row < UNIT // 2, b, a)
    real = row % (UNIT // 2) < ROWS
    parts = [first, second]
    for half in (first, second):
        swapped = pltpu.roll(half, ROWS, 1)
        parts.append(jnp.where(real, -swapped, swapped))
    return jnp.concatenate(parts, axis=2).reshape(v.shape[0], 4 * LANES).astype(BF16)


def collapse(p):
    a = p.reshape(p.shape[0] // UNIT, UNIT, 2 * LANES)
    row = lax.broadcasted_iota(jnp.int32, (a.shape[0], UNIT, LANES), 1)
    return jnp.where(row < UNIT // 2, a[:, :, :LANES], a[:, :, LANES:]).reshape(p.shape[0], LANES)


def beside(m):
    half = m.shape[0] // 2
    return jnp.concatenate([m, jnp.concatenate([-m[half:], m[:half]], axis=0)], axis=1)


def kernel(
    leafs, sweeps, rhs_ref, inc_ref, finv_hbm, coup_hbm, upd_hbm, own_ref, front_ref, out_ref,
    finv, coup, upd, above, comp_d, comp_u, place, take, rhs_s, rhs_u, contrib, rest, back, above_field,
    sent, got, last, told, heard,
    load_sem, above_send, above_recv, field_send, field_recv, back_send, back_recv, sent_sem, got_sem, last_sem,
    told_sem, heard_sem,
):
    fronts, total_rows, doubled = rhs_ref.shape[1:]
    width = doubled // 2
    blocks = own_ref.shape[0]
    groups = total_rows // ROWS
    pairs = fronts * blocks
    top = sweeps - 1
    me = lax.axis_index("leaf")
    level = lax.axis_index("sweep")

    def load(which, i):
        source, target = ((finv_hbm, finv), (coup_hbm, coup), (upd_hbm, upd))[which]
        return pltpu.make_async_copy(source.at[i], target.at[i], load_sem.at[which, i])

    for i in range(fronts):
        load(0, i).start()
    for i in range(fronts):
        load(1, i).start()
        load(2, i).start()

    barrier = pltpu.get_barrier_semaphore()

    @pl.when(level > 0)
    def _():
        for to in range(leafs):
            pl.semaphore_signal(barrier, inc=1, device_id=(level - 1, to), device_id_type=MESH)

    @pl.when(level < top)
    def _():
        pl.semaphore_signal(barrier, inc=1, device_id=(level + 1, me), device_id_type=MESH)

    @pl.when(level == top)
    def _():
        for off in range(1, leafs):
            pl.semaphore_signal(barrier, inc=1, device_id=(level, lax.rem(me + off, leafs)), device_id_type=MESH)

    lane = lax.broadcasted_iota(jnp.int32, (fronts, pairs * UNIT), 1)
    sub = lax.broadcasted_iota(jnp.int32, (fronts, pairs * UNIT), 0)
    lane_front = lane // (blocks * UNIT)
    lane_block = (lane // UNIT) % blocks
    own = own_ref[...].T
    front = front_ref[...].T
    own_l = jnp.zeros_like(lane)
    front_l = jnp.zeros_like(lane)
    for k in range(blocks):
        here = (lane_block == k) & (lane_front == sub)
        own_l += jnp.where(here, own[:, k : k + 1], 0)
        front_l += jnp.where(here, front[:, k : k + 1] + 1, 0)
    own_l = jnp.sum(own_l, axis=0, keepdims=True)
    front_l = jnp.sum(front_l, axis=0, keepdims=True)
    rank = jnp.zeros_like(lane)
    for k in range(blocks):
        rank += jnp.where((own[:, k : k + 1] == own_l) & (sub < lane_front), 1, 0)
    rank = jnp.sum(rank, axis=0, keepdims=True)
    goal = (own_l * SLOTS + rank) * UNIT + lane[:1] % UNIT
    row = lax.broadcasted_iota(jnp.int32, (leafs * PER, pairs * UNIT), 0)
    hot = row == goal
    place[...] = jnp.where(hot, 1.0, 0.0).astype(BF16)
    labels = jnp.where(hot, front_l.astype(F32), 0.0).astype(BF16)
    told[...] = dot(labels, jnp.ones((pairs * UNIT, LANES), BF16)).astype(BF16)

    waits = jnp.where(level < top, leafs, leafs - 1) + jnp.where(level > 0, 1, 0)
    pl.semaphore_wait(barrier, waits)

    leaf_z = leafs // LEAF_X
    steps = [(dz, dx) for dz in range(leaf_z) for dx in range(LEAF_X)]
    steps.sort(key=lambda d: -min(d[0], leaf_z - d[0]) - min(d[1], LEAF_X - d[1]))

    mine = pl.ds(pl.multiple_of(me * PER, PER), PER)

    def spread(source, target, sends, recvs, to_level, offsets):
        for dz, dx in offsets:
            to = lax.rem(me // LEAF_X + dz, leaf_z) * LEAF_X + lax.rem(me % LEAF_X + dx, LEAF_X)
            pltpu.make_async_remote_copy(
                src_ref=source.at[pl.ds(pl.multiple_of(to * PER, PER), PER)],
                dst_ref=target.at[mine],
                send_sem=sends,
                recv_sem=recvs,
                device_id=(to_level, to),
                device_id_type=MESH,
            ).start()

    def wait_for(ref, sem):
        pltpu.make_async_copy(ref, ref, sem).wait()

    def others(ref):
        return ref.at[pl.ds(0, (leafs - 1) * PER)]

    def hand(source, target, send, recv, to_level):
        return pltpu.make_async_remote_copy(
            src_ref=source,
            dst_ref=target,
            send_sem=send,
            recv_sem=recv,
            device_id=(to_level, me),
            device_id_type=MESH,
        )

    def hand_inverse(i):
        return hand(finv_hbm.at[i], above.at[i], above_send.at[i], above_recv.at[i], level + 1)

    def hand_field(g):
        return hand(rhs_s.at[g], above_field.at[g], field_send.at[g], field_recv.at[g], level + 1)

    def hand_back(g):
        return hand(rest.at[g], back.at[g], back_send.at[g], back_recv.at[g], level - 1)

    @pl.when(level < top)
    def _():
        for i in range(fronts):
            hand_inverse(i).start()
        spread(told, heard, told_sem, heard_sem, level + 1, steps)

    def packed_place(index):
        at = (index // ROWS) % 2 * 2 + (index // (2 * ROWS)) % 2
        return at * total_rows + (index // UNIT) * ROWS + index % ROWS

    spots = groups * UNIT
    square_row = lax.broadcasted_iota(jnp.int32, (spots, spots), 0)
    square_col = lax.broadcasted_iota(jnp.int32, (spots, spots), 1)

    def packed(value):
        regroup = jnp.where(square_col == packed_place(square_row), 1.0, 0.0).astype(BF16)
        parts = [value[:, t * LANES : (t + 1) * LANES] for t in range(doubled // LANES)]
        return dot(regroup, jnp.concatenate(parts, axis=0))

    def apply(v, m):
        return collapse(dot(expand(v), m))

    def flat(ref, *at):
        return ref[at].reshape(2 * width, width)

    def rounded(v):
        return v.astype(BF16).astype(F32)

    starts = jnp.where(level == 0, 1.0, 0.0).astype(F32)

    def begin(b, carry):
        these = [b * TOGETHER + n for n in range(TOGETHER)]
        for i in these:
            for which in range(3):
                load(which, i).wait()
        entering = [expand(packed(inc_ref[i])) for i in these]
        fields = [packed(rhs_ref[0, i]) for i in these]
        fields = [
            field - starts * collapse(dot(x, flat(coup, i))) for i, x, field in zip(these, entering, fields)
        ]
        firsts = [expand(rounded(apply(rounded(field), flat(finv, i)))) for i, field in zip(these, fields)]
        for i, field in zip(these, fields):
            at_i = pl.ds(pl.multiple_of(i * UNIT, UNIT), UNIT)
            for g in range(groups):
                rhs_s[g, at_i, :] = field[g * UNIT : (g + 1) * UNIT]
        for i, first in zip(these, firsts):
            for k in range(blocks):
                part = collapse(dot(first, flat(upd, i, k)))
                at_ik = pl.ds(pl.multiple_of((i * blocks + k) * UNIT, UNIT), UNIT)
                for g in range(groups):
                    rhs_u[g, at_ik, :] = part[g * UNIT : (g + 1) * UNIT]
        return carry

    lax.fori_loop(0, fronts // TOGETHER, begin, 0)

    def compose(i, carry):
        wait_for(above.at[i], above_recv.at[i])
        d = dot(beside(flat(above, i)), flat(coup, i)).astype(BF16)
        comp_d[i] = d
        e = beside(dot(beside(d), flat(finv, i)).astype(BF16))
        for k in range(blocks):
            comp_u[i, :, k * width : (k + 1) * width] = dot(e, flat(upd, i, k)).astype(BF16)
        return carry

    @pl.when(level > 0)
    def _():
        lax.fori_loop(0, fronts, compose, 0)

    @pl.when(level > 0)
    def _():
        wait_for(heard, heard_sem)
        h = heard[...].astype(F32)
        t_row = lax.broadcasted_iota(jnp.int32, h.shape, 0)
        t_lane = lax.broadcasted_iota(jnp.int32, h.shape, 1)
        fits = (h == (t_lane // UNIT + 1).astype(F32)) & (t_row % UNIT == t_lane % UNIT)
        take[...] = jnp.where(fits, 1.0, 0.0).T.astype(BF16)[: fronts * UNIT]

    def step(g):
        @pl.when(level == 0)
        def _():
            contrib[...] = rhs_u[g].astype(BF16)

        @pl.when(level > 0)
        def _():
            wait_for(above_field.at[g], field_recv.at[g])
            wait_for(got.at[g], got_sem.at[g])
            rest[g] = (above_field[g] - dot(take[...], got[g])).astype(BF16)
            hand_back(g).start()
            x = expand(rest[g].astype(F32))
            values = []
            for i in range(fronts):
                wide = dot(x[i * UNIT : (i + 1) * UNIT], comp_u[i])
                for k in range(blocks):
                    at = (i * blocks + k) * UNIT
                    values.append(rhs_u[g, at : at + UNIT, :] - collapse(wide[:, k * width : (k + 1) * width]))
            contrib[...] = jnp.concatenate(values, axis=0).astype(BF16)

        sent[g] = dot(place[...], contrib[...]).astype(BF16)

        @pl.when(level < top)
        def _():
            spread(sent.at[g], got.at[g], sent_sem.at[g], got_sem.at[g], level + 1, steps)

        @pl.when(level == top)
        def _():
            spread(sent.at[g], last.at[g], sent_sem.at[g], last_sem.at[g], level, steps[:-1])
            last[g, mine, :] = sent[g, mine, :]

        @pl.when(level > 0)
        def _():
            x = expand(rest[g].astype(F32))
            for i in range(fronts):
                at = i * UNIT
                value = collapse(dot(x[at : at + UNIT], comp_d[i]))
                rhs_s[g, at : at + UNIT, :] = rhs_s[g, at : at + UNIT, :] - value

        @pl.when(level < top)
        def _():
            hand_field(g).start()

    def close(g):
        wait_for(others(last.at[g]), last_sem.at[g])
        back[g] = (rhs_s[g] - dot(take[...], last[g])).astype(BF16)

    def advance(g, carry):
        step(g)

        @pl.when((level == top) & (g >= SKEW))
        def _():
            close(g - SKEW)

        return carry

    lax.fori_loop(0, groups, advance, 0)

    @pl.when(level == top)
    def _():
        for g in range(groups - SKEW, groups):
            close(g)

    @pl.when(level < top)
    def _():
        for g in range(groups):
            wait_for(back.at[g], back_recv.at[g])

    ungroup = jnp.where(square_row == packed_place(square_col), 1.0, 0.0).astype(BF16)
    for i in range(fronts):
        at = i * UNIT
        value = jnp.concatenate([back[g].astype(F32)[at : at + UNIT] for g in range(groups)], axis=0)
        solved = apply(value, flat(finv, i)).astype(BF16)
        value = dot(ungroup, solved).astype(BF16)
        for t in range(doubled // LANES):
            out_ref[0, i, :, t * LANES : (t + 1) * LANES] = value[t * total_rows : (t + 1) * total_rows]

    @pl.when(level < top)
    def _():
        wait_for(told, told_sem)
        for i in range(fronts):
            hand_inverse(i).wait_send()

        def drain(g, carry):
            wait_for(sent.at[g], sent_sem.at[g])
            hand_field(g).wait_send()
            return carry

        lax.fori_loop(0, groups, drain, 0)

    @pl.when(level > 0)
    def _():
        def drain(g, carry):
            hand_back(g).wait_send()
            return carry

        lax.fori_loop(0, groups, drain, 0)

    @pl.when(level == top)
    def _():
        def drain(g, carry):
            wait_for(others(sent.at[g]), sent_sem.at[g])
            return carry

        lax.fori_loop(0, groups, drain, 0)


def body(leafs, sweeps, rhs, incoming, front_inv, coupling, update, dest_owner, dest_front):
    fronts, total_rows, doubled = incoming.shape
    width = doubled // 2
    blocks = dest_owner.shape[1]
    groups = total_rows // ROWS
    slots = leafs * PER
    pairs = fronts * blocks
    vmem = pl.BlockSpec(memory_space=pltpu.VMEM)
    hbm = pl.BlockSpec(memory_space=pl.ANY)
    dma = pltpu.SemaphoreType.DMA
    return pl.pallas_call(
        functools.partial(kernel, leafs, sweeps),
        out_shape=jax.ShapeDtypeStruct(rhs.shape, BF16),
        in_specs=[vmem, vmem, hbm, hbm, hbm, vmem, vmem],
        out_specs=vmem,
        scratch_shapes=[
            pltpu.VMEM(front_inv.shape[1:], BF16),
            pltpu.VMEM(coupling.shape[1:], BF16),
            pltpu.VMEM(update.shape[1:], BF16),
            pltpu.VMEM(front_inv.shape[1:], BF16),
            pltpu.VMEM((fronts, 2 * width, width), BF16),
            pltpu.VMEM((fronts, 2 * width, blocks * width), BF16),
            pltpu.VMEM((slots, pairs * UNIT), BF16),
            pltpu.VMEM((fronts * UNIT, slots), BF16),
            pltpu.VMEM((groups, fronts * UNIT, LANES), F32),
            pltpu.VMEM((groups, pairs * UNIT, LANES), F32),
            pltpu.VMEM((pairs * UNIT, LANES), BF16),
            pltpu.VMEM((groups, fronts * UNIT, LANES), BF16),
            pltpu.VMEM((groups, fronts * UNIT, LANES), BF16),
            pltpu.VMEM((groups, fronts * UNIT, LANES), F32),
            pltpu.VMEM((groups, slots, LANES), BF16),
            pltpu.VMEM((groups, slots, LANES), BF16),
            pltpu.VMEM((groups, slots, LANES), BF16),
            pltpu.VMEM((slots, LANES), BF16),
            pltpu.VMEM((slots, LANES), BF16),
            dma((3, fronts)),
            dma((fronts,)),
            dma((fronts,)),
            dma((groups,)),
            dma((groups,)),
            dma((groups,)),
            dma((groups,)),
            dma((groups,)),
            dma((groups,)),
            dma((groups,)),
            dma,
            dma,
        ],
        compiler_params=pltpu.CompilerParams(
            collective_id=0, has_side_effects=True, vmem_limit_bytes=60 * 1024 * 1024
        ),
    )(rhs, incoming, front_inv[0], coupling[0], update[0], dest_owner.T, dest_front.T)


def solution(mesh):
    return jax.shard_map(
        functools.partial(body, mesh.shape["leaf"], mesh.shape["sweep"]),
        mesh=mesh,
        in_specs=(
            P("sweep", "leaf", None, None),
            P("leaf", None, None),
            P("sweep", "leaf", None, None, None),
            P("sweep", "leaf", None, None, None),
            P("sweep", "leaf", None, None, None, None),
            P("leaf", None),
            P("leaf", None),
        ),
        out_specs=P("sweep", "leaf", None, None),
        check_vma=False,
    )
```

```python
import functools

import jax
import jax.numpy as jnp
from jax import lax
from jax.experimental import pallas as pl
from jax.experimental.pallas import tpu as pltpu
from jax.sharding import PartitionSpec as P

ROWS = 2
SLOTS = 2
LANES = 128
TOGETHER = 4
LEAF_X = 4
UNIT = 8
PER = SLOTS * UNIT
SKEW = 2
HANDED = 1
MESH = pl.DeviceIdType.MESH
F32 = jnp.float32
BF16 = jnp.bfloat16


def dot(a, b):
    return jnp.dot(a, b, preferred_element_type=F32)


def expand(v):
    a = v.reshape(v.shape[0] // UNIT, UNIT, LANES)
    b = pltpu.roll(a, UNIT // 2, 1)
    row = lax.broadcasted_iota(jnp.int32, a.shape, 1)
    first = jnp.where(row < UNIT // 2, a, b)
    second = jnp.where(row < UNIT // 2, b, a)
    real = row % (UNIT // 2) < ROWS
    parts = [first, second]
    for half in (first, second):
        swapped = pltpu.roll(half, ROWS, 1)
        parts.append(jnp.where(real, -swapped, swapped))
    return jnp.concatenate(parts, axis=2).reshape(v.shape[0], 4 * LANES).astype(BF16)


def collapse(p):
    a = p.reshape(p.shape[0] // UNIT, UNIT, 2 * LANES)
    row = lax.broadcasted_iota(jnp.int32, (a.shape[0], UNIT, LANES), 1)
    return jnp.where(row < UNIT // 2, a[:, :, :LANES], a[:, :, LANES:]).reshape(p.shape[0], LANES)


def beside(m):
    half = m.shape[0] // 2
    return jnp.concatenate([m, jnp.concatenate([-m[half:], m[:half]], axis=0)], axis=1)


def kernel(
    leafs, sweeps, rhs_ref, inc_ref, finv_hbm, coup_hbm, upd_hbm, own_ref, front_ref, out_ref,
    finv, coup, upd, above, comp_d, comp_u, place, take, rhs_s, rhs_u, contrib, rest, back, above_field,
    result, solved, entered, sent, got, last, told, heard,
    load_sem, above_send, above_recv, field_send, field_recv, back_send, back_recv, solved_send, entered_recv, sent_sem, got_sem, last_sem,
    told_sem, heard_sem,
):
    fronts, total_rows, doubled = rhs_ref.shape[1:]
    width = doubled // 2
    blocks = own_ref.shape[0]
    groups = total_rows // ROWS
    pairs = fronts * blocks
    top = sweeps - 1
    me = lax.axis_index("leaf")
    level = lax.axis_index("sweep")
    kept = (level == HANDED) | (level == top)
    entry = level == HANDED + 1
    fused = (level > 0) & (level != HANDED + 1)

    def load(which, i):
        source, target = ((finv_hbm, finv), (coup_hbm, coup), (upd_hbm, upd))[which]
        return pltpu.make_async_copy(source.at[i], target.at[i], load_sem.at[which, i])

    for i in range(fronts):
        load(0, i).start()
    for i in range(fronts):
        load(1, i).start()
        load(2, i).start()

    barrier = pltpu.get_barrier_semaphore()

    @pl.when(fused)
    def _():
        for to in range(leafs):
            pl.semaphore_signal(barrier, inc=1, device_id=(level - 1, to), device_id_type=MESH)

    @pl.when(entry)
    def _():
        pl.semaphore_signal(barrier, inc=1, device_id=(level - 1, me), device_id_type=MESH)

    @pl.when(jnp.logical_not(kept))
    def _():
        pl.semaphore_signal(barrier, inc=1, device_id=(level + 1, me), device_id_type=MESH)

    @pl.when(kept)
    def _():
        for off in range(1, leafs):
            pl.semaphore_signal(barrier, inc=1, device_id=(level, lax.rem(me + off, leafs)), device_id_type=MESH)

    lane = lax.broadcasted_iota(jnp.int32, (fronts, pairs * UNIT), 1)
    sub = lax.broadcasted_iota(jnp.int32, (fronts, pairs * UNIT), 0)
    lane_front = lane // (blocks * UNIT)
    lane_block = (lane // UNIT) % blocks
    own = own_ref[...].T
    front = front_ref[...].T
    own_l = jnp.zeros_like(lane)
    front_l = jnp.zeros_like(lane)
    for k in range(blocks):
        here = (lane_block == k) & (lane_front == sub)
        own_l += jnp.where(here, own[:, k : k + 1], 0)
        front_l += jnp.where(here, front[:, k : k + 1] + 1, 0)
    own_l = jnp.sum(own_l, axis=0, keepdims=True)
    front_l = jnp.sum(front_l, axis=0, keepdims=True)
    rank = jnp.zeros_like(lane)
    for k in range(blocks):
        rank += jnp.where((own[:, k : k + 1] == own_l) & (sub < lane_front), 1, 0)
    rank = jnp.sum(rank, axis=0, keepdims=True)
    goal = (own_l * SLOTS + rank) * UNIT + lane[:1] % UNIT
    row = lax.broadcasted_iota(jnp.int32, (leafs * PER, pairs * UNIT), 0)
    hot = row == goal
    place[...] = jnp.where(hot, 1.0, 0.0).astype(BF16)
    labels = jnp.where(hot, front_l.astype(F32), 0.0).astype(BF16)
    told[...] = dot(labels, jnp.ones((pairs * UNIT, LANES), BF16)).astype(BF16)

    waits = jnp.where(kept, leafs - 1, leafs) + jnp.where(fused, 1, 0) + jnp.where(level == HANDED, 1, 0)
    pl.semaphore_wait(barrier, waits)

    leaf_z = leafs // LEAF_X
    steps = [(dz, dx) for dz in range(leaf_z) for dx in range(LEAF_X)]
    steps.sort(key=lambda d: -min(d[0], leaf_z - d[0]) - min(d[1], LEAF_X - d[1]))

    mine = pl.ds(pl.multiple_of(me * PER, PER), PER)

    def spread(source, target, sends, recvs, to_level, offsets):
        for dz, dx in offsets:
            to = lax.rem(me // LEAF_X + dz, leaf_z) * LEAF_X + lax.rem(me % LEAF_X + dx, LEAF_X)
            pltpu.make_async_remote_copy(
                src_ref=source.at[pl.ds(pl.multiple_of(to * PER, PER), PER)],
                dst_ref=target.at[mine],
                send_sem=sends,
                recv_sem=recvs,
                device_id=(to_level, to),
                device_id_type=MESH,
            ).start()

    def wait_for(ref, sem):
        pltpu.make_async_copy(ref, ref, sem).wait()

    def others(ref):
        return ref.at[pl.ds(0, (leafs - 1) * PER)]

    def hand(source, target, send, recv, to_level):
        return pltpu.make_async_remote_copy(
            src_ref=source,
            dst_ref=target,
            send_sem=send,
            recv_sem=recv,
            device_id=(to_level, me),
            device_id_type=MESH,
        )

    def hand_inverse(i):
        return hand(finv_hbm.at[i], above.at[i], above_send.at[i], above_recv.at[i], level + 1)

    def hand_field(g):
        return hand(rhs_s.at[g], above_field.at[g], field_send.at[g], field_recv.at[g], level + 1)

    def hand_solved(g):
        return hand(solved.at[g], entered.at[g], solved_send.at[g], entered_recv.at[g], level + 1)

    def hand_back(g):
        return hand(rest.at[g], back.at[g], back_send.at[g], back_recv.at[g], level - 1)

    @pl.when(jnp.logical_not(kept))
    def _():
        for i in range(fronts):
            hand_inverse(i).start()
        spread(told, heard, told_sem, heard_sem, level + 1, steps)

    def packed_place(index):
        at = (index // ROWS) % 2 * 2 + (index // (2 * ROWS)) % 2
        return at * total_rows + (index // UNIT) * ROWS + index % ROWS

    spots = groups * UNIT
    square_row = lax.broadcasted_iota(jnp.int32, (spots, spots), 0)
    square_col = lax.broadcasted_iota(jnp.int32, (spots, spots), 1)

    def packed(value):
        regroup = jnp.where(square_col == packed_place(square_row), 1.0, 0.0).astype(BF16)
        parts = [value[:, t * LANES : (t + 1) * LANES] for t in range(doubled // LANES)]
        return dot(regroup, jnp.concatenate(parts, axis=0))

    def apply(v, m):
        return collapse(dot(expand(v), m))

    def flat(ref, *at):
        return ref[at].reshape(2 * width, width)

    def rounded(v):
        return v.astype(BF16).astype(F32)

    starts = jnp.where(level == 0, 1.0, 0.0).astype(F32)

    def begin(b, carry):
        these = [b * TOGETHER + n for n in range(TOGETHER)]
        for i in these:
            for which in range(3):
                load(which, i).wait()
        entering = [expand(packed(inc_ref[i])) for i in these]
        fields = [packed(rhs_ref[0, i]) for i in these]
        fields = [
            field - starts * collapse(dot(x, flat(coup, i))) for i, x, field in zip(these, entering, fields)
        ]
        firsts = [expand(rounded(apply(rounded(field), flat(finv, i)))) for i, field in zip(these, fields)]
        for i, field in zip(these, fields):
            at_i = pl.ds(pl.multiple_of(i * UNIT, UNIT), UNIT)
            for g in range(groups):
                rhs_s[g, at_i, :] = field[g * UNIT : (g + 1) * UNIT]
        for i, first in zip(these, firsts):
            for k in range(blocks):
                part = collapse(dot(first, flat(upd, i, k)))
                at_ik = pl.ds(pl.multiple_of((i * blocks + k) * UNIT, UNIT), UNIT)
                for g in range(groups):
                    rhs_u[g, at_ik, :] = part[g * UNIT : (g + 1) * UNIT]
        return carry

    lax.fori_loop(0, fronts // TOGETHER, begin, 0)

    def compose(b, carry):
        these = [b * TOGETHER + n for n in range(TOGETHER)]
        for i in these:
            @pl.when(fused)
            def _():
                wait_for(above.at[i], above_recv.at[i])

            @pl.when(entry)
            def _():
                unit_row = lax.broadcasted_iota(jnp.int32, (width, width), 0)
                unit_col = lax.broadcasted_iota(jnp.int32, (width, width), 1)
                above[i, 0] = jnp.where(unit_row == unit_col, 1.0, 0.0).astype(BF16)
                above[i, 1] = jnp.zeros((width, width), BF16)

        downs = [dot(beside(flat(above, i)), flat(coup, i)).astype(BF16) for i in these]
        for i, down in zip(these, downs):
            comp_d[i] = down
        firsts = [beside(dot(beside(down), flat(finv, i)).astype(BF16)) for i, down in zip(these, downs)]
        for k in range(blocks):
            for i, first in zip(these, firsts):
                comp_u[i, :, k * width : (k + 1) * width] = dot(first, flat(upd, i, k)).astype(BF16)
        return carry

    @pl.when(level > 0)
    def _():
        lax.fori_loop(0, fronts // TOGETHER, compose, 0)

    @pl.when(fused)
    def _():
        wait_for(heard, heard_sem)
        h = heard[...].astype(F32)
        t_row = lax.broadcasted_iota(jnp.int32, h.shape, 0)
        t_lane = lax.broadcasted_iota(jnp.int32, h.shape, 1)
        fits = (h == (t_lane // UNIT + 1).astype(F32)) & (t_row % UNIT == t_lane % UNIT)
        take[...] = jnp.where(fits, 1.0, 0.0).T.astype(BF16)[: fronts * UNIT]

    def step(g):
        @pl.when(level == 0)
        def _():
            contrib[...] = rhs_u[g].astype(BF16)

        @pl.when(level > 0)
        def _():
            @pl.when(fused)
            def _():
                wait_for(above_field.at[g], field_recv.at[g])
                wait_for(got.at[g], got_sem.at[g])
                rest[g] = (above_field[g] - dot(take[...], got[g])).astype(BF16)
                hand_back(g).start()

            @pl.when(entry)
            def _():
                wait_for(entered.at[g], entered_recv.at[g])
                rest[g] = entered[g]

            x = expand(rest[g].astype(F32))
            values = []
            for i in range(fronts):
                wide = dot(x[i * UNIT : (i + 1) * UNIT], comp_u[i])
                for k in range(blocks):
                    at = (i * blocks + k) * UNIT
                    values.append(rhs_u[g, at : at + UNIT, :] - collapse(wide[:, k * width : (k + 1) * width]))
            contrib[...] = jnp.concatenate(values, axis=0).astype(BF16)

        sent[g] = dot(place[...], contrib[...]).astype(BF16)

        @pl.when(jnp.logical_not(kept))
        def _():
            spread(sent.at[g], got.at[g], sent_sem.at[g], got_sem.at[g], level + 1, steps)

        @pl.when(kept)
        def _():
            spread(sent.at[g], last.at[g], sent_sem.at[g], last_sem.at[g], level, steps[:-1])
            last[g, mine, :] = sent[g, mine, :]

        @pl.when(level > 0)
        def _():
            x = expand(rest[g].astype(F32))
            for i in range(fronts):
                at = i * UNIT
                value = collapse(dot(x[at : at + UNIT], comp_d[i]))
                rhs_s[g, at : at + UNIT, :] = rhs_s[g, at : at + UNIT, :] - value

        @pl.when(jnp.logical_not(kept))
        def _():
            hand_field(g).start()

    def close(g):
        wait_for(others(last.at[g]), last_sem.at[g])
        value = (rhs_s[g] - dot(take[...], last[g])).astype(BF16)
        x = expand(value.astype(F32))
        at_g = pl.ds(pl.multiple_of(g * UNIT, UNIT), UNIT)
        values = []
        for i in range(fronts):
            value = collapse(dot(x[i * UNIT : (i + 1) * UNIT], flat(finv, i)))
            result[i, at_g, :] = value
            values.append(value)

        @pl.when(level == HANDED)
        def _():
            solved[g] = jnp.concatenate(values, axis=0).astype(BF16)
            hand_solved(g).start()

    def advance(g, carry):
        step(g)

        @pl.when(kept & (g >= SKEW))
        def _():
            close(g - SKEW)

        return carry

    lax.fori_loop(0, groups, advance, 0)

    @pl.when(kept)
    def _():
        def finish(g, carry):
            close(g)
            return carry

        lax.fori_loop(groups - SKEW, groups, finish, 0)

    @pl.when(jnp.logical_not(kept))
    def _():
        for g in range(groups):
            wait_for(back.at[g], back_recv.at[g])
        for i in range(fronts):
            at = i * UNIT
            value = jnp.concatenate([back[g].astype(F32)[at : at + UNIT] for g in range(groups)], axis=0)
            result[i] = apply(value, flat(finv, i))

    ungroup = jnp.where(square_row == packed_place(square_col), 1.0, 0.0).astype(BF16)
    for i in range(fronts):
        value = dot(ungroup, result[i].astype(BF16)).astype(BF16)
        for t in range(doubled // LANES):
            out_ref[0, i, :, t * LANES : (t + 1) * LANES] = value[t * total_rows : (t + 1) * total_rows]

    @pl.when(jnp.logical_not(kept))
    def _():
        wait_for(told, told_sem)
        for i in range(fronts):
            hand_inverse(i).wait_send()

        def drain(g, carry):
            wait_for(sent.at[g], sent_sem.at[g])
            hand_field(g).wait_send()
            return carry

        lax.fori_loop(0, groups, drain, 0)

    @pl.when(fused)
    def _():
        def drain(g, carry):
            hand_back(g).wait_send()
            return carry

        lax.fori_loop(0, groups, drain, 0)

    @pl.when(kept)
    def _():
        def drain(g, carry):
            wait_for(others(sent.at[g]), sent_sem.at[g])
            return carry

        lax.fori_loop(0, groups, drain, 0)

    @pl.when(level == HANDED)
    def _():
        def drain(g, carry):
            hand_solved(g).wait_send()
            return carry

        lax.fori_loop(0, groups, drain, 0)


def body(leafs, sweeps, rhs, incoming, front_inv, coupling, update, dest_owner, dest_front):
    fronts, total_rows, doubled = incoming.shape
    width = doubled // 2
    blocks = dest_owner.shape[1]
    groups = total_rows // ROWS
    slots = leafs * PER
    pairs = fronts * blocks
    vmem = pl.BlockSpec(memory_space=pltpu.VMEM)
    hbm = pl.BlockSpec(memory_space=pl.ANY)
    dma = pltpu.SemaphoreType.DMA
    return pl.pallas_call(
        functools.partial(kernel, leafs, sweeps),
        out_shape=jax.ShapeDtypeStruct(rhs.shape, BF16),
        in_specs=[vmem, vmem, hbm, hbm, hbm, vmem, vmem],
        out_specs=vmem,
        scratch_shapes=[
            pltpu.VMEM(front_inv.shape[1:], BF16),
            pltpu.VMEM(coupling.shape[1:], BF16),
            pltpu.VMEM(update.shape[1:], BF16),
            pltpu.VMEM(front_inv.shape[1:], BF16),
            pltpu.VMEM((fronts, 2 * width, width), BF16),
            pltpu.VMEM((fronts, 2 * width, blocks * width), BF16),
            pltpu.VMEM((slots, pairs * UNIT), BF16),
            pltpu.VMEM((fronts * UNIT, slots), BF16),
            pltpu.VMEM((groups, fronts * UNIT, LANES), F32),
            pltpu.VMEM((groups, pairs * UNIT, LANES), F32),
            pltpu.VMEM((pairs * UNIT, LANES), BF16),
            pltpu.VMEM((groups, fronts * UNIT, LANES), BF16),
            pltpu.VMEM((groups, fronts * UNIT, LANES), BF16),
            pltpu.VMEM((groups, fronts * UNIT, LANES), F32),
            pltpu.VMEM((fronts, groups * UNIT, LANES), F32),
            pltpu.VMEM((groups, fronts * UNIT, LANES), BF16),
            pltpu.VMEM((groups, fronts * UNIT, LANES), BF16),
            pltpu.VMEM((groups, slots, LANES), BF16),
            pltpu.VMEM((groups, slots, LANES), BF16),
            pltpu.VMEM((groups, slots, LANES), BF16),
            pltpu.VMEM((slots, LANES), BF16),
            pltpu.VMEM((slots, LANES), BF16),
            dma((3, fronts)),
            dma((fronts,)),
            dma((fronts,)),
            dma((groups,)),
            dma((groups,)),
            dma((groups,)),
            dma((groups,)),
            dma((groups,)),
            dma((groups,)),
            dma((groups,)),
            dma((groups,)),
            dma((groups,)),
            dma,
            dma,
        ],
        compiler_params=pltpu.CompilerParams(
            collective_id=0, has_side_effects=True, vmem_limit_bytes=60 * 1024 * 1024
        ),
    )(rhs, incoming, front_inv[0], coupling[0], update[0], dest_owner.T, dest_front.T)


def solution(mesh):
    return jax.shard_map(
        functools.partial(body, mesh.shape["leaf"], mesh.shape["sweep"]),
        mesh=mesh,
        in_specs=(
            P("sweep", "leaf", None, None),
            P("leaf", None, None),
            P("sweep", "leaf", None, None, None),
            P("sweep", "leaf", None, None, None),
            P("sweep", "leaf", None, None, None, None),
            P("leaf", None),
            P("leaf", None),
        ),
        out_specs=P("sweep", "leaf", None, None),
        check_vma=False,
    )
```

```python
import functools

import jax
import jax.numpy as jnp
from jax import lax
from jax.experimental import pallas as pl
from jax.experimental.pallas import tpu as pltpu
from jax.sharding import PartitionSpec as P

ROWS = 2
SLOTS = 2
LANES = 128
TOGETHER = 4
LEAF_X = 4
UNIT = 8
PER = SLOTS * UNIT
SKEW = 2
WINDOW = 4
HANDED = 1
MESH = pl.DeviceIdType.MESH
F32 = jnp.float32
BF16 = jnp.bfloat16


def dot(a, b):
    return jnp.dot(a, b, preferred_element_type=F32)


def expand(v):
    a = v.reshape(v.shape[0] // UNIT, UNIT, LANES)
    b = pltpu.roll(a, UNIT // 2, 1)
    row = lax.broadcasted_iota(jnp.int32, a.shape, 1)
    first = jnp.where(row < UNIT // 2, a, b)
    second = jnp.where(row < UNIT // 2, b, a)
    real = row % (UNIT // 2) < ROWS
    parts = [first, second]
    for half in (first, second):
        swapped = pltpu.roll(half, ROWS, 1)
        parts.append(jnp.where(real, -swapped, swapped))
    return jnp.concatenate(parts, axis=2).reshape(v.shape[0], 4 * LANES).astype(BF16)


def collapse(p):
    a = p.reshape(p.shape[0] // UNIT, UNIT, 2 * LANES)
    row = lax.broadcasted_iota(jnp.int32, (a.shape[0], UNIT, LANES), 1)
    return jnp.where(row < UNIT // 2, a[:, :, :LANES], a[:, :, LANES:]).reshape(p.shape[0], LANES)


def beside(m):
    half = m.shape[0] // 2
    return jnp.concatenate([m, jnp.concatenate([-m[half:], m[:half]], axis=0)], axis=1)


def kernel(
    leafs, sweeps, rhs_hbm, inc_hbm, finv_hbm, coup_hbm, upd_hbm, own_ref, front_ref, out_ref,
    rhs_ref, inc_ref, finv, coup, upd, above, comp_d, comp_u, place, take, rhs_s, rhs_u, rest, back, above_field,
    result, solved, entered, sent, got, last, told, heard,
    load_sem, above_send, above_recv, field_send, field_recv, back_send, back_recv, solved_send, entered_recv, sent_sem, got_sem, last_sem,
    told_sem, heard_sem,
):
    fronts, total_rows, doubled = inc_ref.shape
    width = doubled // 2
    blocks = own_ref.shape[0]
    groups = total_rows // ROWS
    pairs = fronts * blocks
    top = sweeps - 1
    me = lax.axis_index("leaf")
    level = lax.axis_index("sweep")
    kept = (level == HANDED) | (level == top)
    entry = level == HANDED + 1
    fused = (level > 0) & (level != HANDED + 1)

    def load(which, i):
        source, target = ((finv_hbm, finv), (coup_hbm, coup), (upd_hbm, upd), (rhs_hbm, rhs_ref), (inc_hbm, inc_ref))[which]
        return pltpu.make_async_copy(source.at[i], target.at[i], load_sem.at[which, i])

    for i in range(fronts):
        for which in (3, 4, 1, 0, 2):
            load(which, i).start()

    barrier = pltpu.get_barrier_semaphore()

    @pl.when(fused)
    def _():
        for to in range(leafs):
            pl.semaphore_signal(barrier, inc=1, device_id=(level - 1, to), device_id_type=MESH)

    @pl.when(entry)
    def _():
        pl.semaphore_signal(barrier, inc=1, device_id=(level - 1, me), device_id_type=MESH)

    @pl.when(jnp.logical_not(kept))
    def _():
        pl.semaphore_signal(barrier, inc=1, device_id=(level + 1, me), device_id_type=MESH)

    @pl.when(kept)
    def _():
        for off in range(1, leafs):
            pl.semaphore_signal(barrier, inc=1, device_id=(level, lax.rem(me + off, leafs)), device_id_type=MESH)

    lane = lax.broadcasted_iota(jnp.int32, (fronts, pairs * UNIT), 1)
    sub = lax.broadcasted_iota(jnp.int32, (fronts, pairs * UNIT), 0)
    lane_front = lane // (blocks * UNIT)
    lane_block = (lane // UNIT) % blocks
    own = own_ref[...].T
    front = front_ref[...].T
    own_l = jnp.zeros_like(lane)
    front_l = jnp.zeros_like(lane)
    for k in range(blocks):
        here = (lane_block == k) & (lane_front == sub)
        own_l += jnp.where(here, own[:, k : k + 1], 0)
        front_l += jnp.where(here, front[:, k : k + 1] + 1, 0)
    own_l = jnp.sum(own_l, axis=0, keepdims=True)
    front_l = jnp.sum(front_l, axis=0, keepdims=True)
    rank = jnp.zeros_like(lane)
    for k in range(blocks):
        rank += jnp.where((own[:, k : k + 1] == own_l) & (sub < lane_front), 1, 0)
    rank = jnp.sum(rank, axis=0, keepdims=True)
    goal = (own_l * SLOTS + rank) * UNIT + lane[:1] % UNIT
    row = lax.broadcasted_iota(jnp.int32, (leafs * PER, pairs * UNIT), 0)
    hot = row == goal
    place[...] = jnp.where(hot, 1.0, 0.0).astype(BF16)
    labels = jnp.where(hot, front_l.astype(F32), 0.0).astype(BF16)
    told[...] = dot(labels, jnp.ones((pairs * UNIT, LANES), BF16)).astype(BF16)

    waits = jnp.where(kept, leafs - 1, leafs) + jnp.where(fused, 1, 0) + jnp.where(level == HANDED, 1, 0)
    pl.semaphore_wait(barrier, waits)

    leaf_z = leafs // LEAF_X
    steps = [(dz, dx) for dz in range(leaf_z) for dx in range(LEAF_X)]
    steps.sort(key=lambda d: -min(d[0], leaf_z - d[0]) - min(d[1], LEAF_X - d[1]))

    mine = pl.ds(pl.multiple_of(me * PER, PER), PER)

    def spread(source, target, sends, recvs, to_level, offsets):
        for dz, dx in offsets:
            to = lax.rem(me // LEAF_X + dz, leaf_z) * LEAF_X + lax.rem(me % LEAF_X + dx, LEAF_X)
            pltpu.make_async_remote_copy(
                src_ref=source.at[pl.ds(pl.multiple_of(to * PER, PER), PER)],
                dst_ref=target.at[mine],
                send_sem=sends,
                recv_sem=recvs,
                device_id=(to_level, to),
                device_id_type=MESH,
            ).start()

    def wait_for(ref, sem):
        pltpu.make_async_copy(ref, ref, sem).wait()

    def others(ref):
        return ref.at[pl.ds(0, (leafs - 1) * PER)]

    def hand(source, target, send, recv, to_level):
        return pltpu.make_async_remote_copy(
            src_ref=source,
            dst_ref=target,
            send_sem=send,
            recv_sem=recv,
            device_id=(to_level, me),
            device_id_type=MESH,
        )

    def hand_inverse(i):
        return hand(finv_hbm.at[i], above.at[i], above_send.at[i], above_recv.at[i], level + 1)

    def hand_field(g):
        return hand(rhs_s.at[g], above_field.at[g], field_send.at[g], field_recv.at[g], level + 1)

    def hand_solved(g):
        return hand(solved.at[g], entered.at[g], solved_send.at[g], entered_recv.at[g], level + 1)

    def hand_back(g):
        return hand(rest.at[g], back.at[g], back_send.at[g], back_recv.at[g], level - 1)

    @pl.when(jnp.logical_not(kept))
    def _():
        for i in range(fronts):
            hand_inverse(i).start()
        spread(told, heard, told_sem, heard_sem, level + 1, steps)

    def packed_place(index):
        at = (index // ROWS) % 2 * 2 + (index // (2 * ROWS)) % 2
        return at * total_rows + (index // UNIT) * ROWS + index % ROWS

    spots = groups * UNIT
    square_row = lax.broadcasted_iota(jnp.int32, (spots, spots), 0)
    square_col = lax.broadcasted_iota(jnp.int32, (spots, spots), 1)

    def packed(value):
        regroup = jnp.where(square_col == packed_place(square_row), 1.0, 0.0).astype(BF16)
        parts = [value[:, t * LANES : (t + 1) * LANES] for t in range(doubled // LANES)]
        return dot(regroup, jnp.concatenate(parts, axis=0))

    def apply(v, m):
        return collapse(dot(expand(v), m))

    def flat(ref, *at):
        return ref[at].reshape(2 * width, width)

    def rounded(v):
        return v.astype(BF16).astype(F32)

    starts = jnp.where(level == 0, 1.0, 0.0).astype(F32)

    def begin(b, carry):
        these = [b * TOGETHER + n for n in range(TOGETHER)]
        for i in these:
            for which in range(5):
                load(which, i).wait()
        entering = [expand(packed(inc_ref[i])) for i in these]
        fields = [packed(rhs_ref[i]) for i in these]
        fields = [
            field - starts * collapse(dot(x, flat(coup, i))) for i, x, field in zip(these, entering, fields)
        ]
        firsts = [expand(rounded(apply(rounded(field), flat(finv, i)))) for i, field in zip(these, fields)]
        for i, field in zip(these, fields):
            at_i = pl.ds(pl.multiple_of(i * UNIT, UNIT), UNIT)
            for g in range(groups):
                rhs_s[g, at_i, :] = field[g * UNIT : (g + 1) * UNIT]
        for i, first in zip(these, firsts):
            for k in range(blocks):
                part = collapse(dot(first, flat(upd, i, k)))
                at_ik = pl.ds(pl.multiple_of((i * blocks + k) * UNIT, UNIT), UNIT)
                for g in range(groups):
                    rhs_u[g, at_ik, :] = part[g * UNIT : (g + 1) * UNIT]
        return carry

    lax.fori_loop(0, fronts // TOGETHER, begin, 0)

    def compose(b, carry):
        these = [b * TOGETHER + n for n in range(TOGETHER)]
        for i in these:
            @pl.when(fused)
            def _():
                wait_for(above.at[i], above_recv.at[i])

            @pl.when(entry)
            def _():
                unit_row = lax.broadcasted_iota(jnp.int32, (width, width), 0)
                unit_col = lax.broadcasted_iota(jnp.int32, (width, width), 1)
                above[i, 0] = jnp.where(unit_row == unit_col, 1.0, 0.0).astype(BF16)
                above[i, 1] = jnp.zeros((width, width), BF16)

        downs = [dot(beside(flat(above, i)), flat(coup, i)).astype(BF16) for i in these]
        for i, down in zip(these, downs):
            comp_d[i] = down
        firsts = [beside(dot(beside(down), flat(finv, i)).astype(BF16)) for i, down in zip(these, downs)]
        for k in range(blocks):
            for i, first in zip(these, firsts):
                comp_u[i, :, k * width : (k + 1) * width] = dot(first, flat(upd, i, k)).astype(BF16)
        return carry

    @pl.when(level > 0)
    def _():
        lax.fori_loop(0, fronts // TOGETHER, compose, 0)

    @pl.when(fused)
    def _():
        wait_for(heard, heard_sem)
        h = heard[...].astype(F32)
        t_row = lax.broadcasted_iota(jnp.int32, h.shape, 0)
        t_lane = lax.broadcasted_iota(jnp.int32, h.shape, 1)
        fits = (h == (t_lane // UNIT + 1).astype(F32)) & (t_row % UNIT == t_lane % UNIT)
        take[...] = jnp.where(fits, 1.0, 0.0).T.astype(BF16)[: fronts * UNIT]

    def step(g):
        @pl.when((level == 0) & (g >= WINDOW))
        def _():
            wait_for(back.at[g - WINDOW], back_recv.at[g - WINDOW])

        @pl.when(level == 0)
        def _():
            sent[g] = dot(place[...], rhs_u[g].astype(BF16)).astype(BF16)

        @pl.when(fused)
        def _():
            wait_for(above_field.at[g], field_recv.at[g])
            wait_for(got.at[g], got_sem.at[g])

        @pl.when(entry)
        def _():
            wait_for(entered.at[g], entered_recv.at[g])

        @pl.when(level > 0)
        def _():
            summed = (above_field[g] - dot(take[...], got[g])).astype(BF16).astype(F32)
            remainder = jnp.where(entry, entered[g].astype(F32), summed)
            rest[g] = remainder.astype(BF16)
            x = expand(remainder)
            values = []
            for i in range(fronts):
                wide = dot(x[i * UNIT : (i + 1) * UNIT], comp_u[i])
                for k in range(blocks):
                    at = (i * blocks + k) * UNIT
                    values.append(rhs_u[g, at : at + UNIT, :] - collapse(wide[:, k * width : (k + 1) * width]))
            contrib = jnp.concatenate(values, axis=0).astype(BF16)
            sent[g] = dot(place[...], contrib).astype(BF16)

        @pl.when(jnp.logical_not(kept))
        def _():
            spread(sent.at[g], got.at[g], sent_sem.at[g], got_sem.at[g], level + 1, steps)

        @pl.when(kept)
        def _():
            spread(sent.at[g], last.at[g], sent_sem.at[g], last_sem.at[g], level, steps[:-1])
            last[g, mine, :] = sent[g, mine, :]

        @pl.when(fused)
        def _():
            hand_back(g).start()

        @pl.when(level > 0)
        def _():
            x = expand(rest[g].astype(F32))
            for i in range(fronts):
                at = i * UNIT
                value = collapse(dot(x[at : at + UNIT], comp_d[i]))
                rhs_s[g, at : at + UNIT, :] = rhs_s[g, at : at + UNIT, :] - value

        @pl.when(jnp.logical_not(kept))
        def _():
            hand_field(g).start()

    def close(g):
        wait_for(others(last.at[g]), last_sem.at[g])
        value = (rhs_s[g] - dot(take[...], last[g])).astype(BF16)
        x = expand(value.astype(F32))
        at_g = pl.ds(pl.multiple_of(g * UNIT, UNIT), UNIT)
        values = []
        for i in range(fronts):
            value = collapse(dot(x[i * UNIT : (i + 1) * UNIT], flat(finv, i)))
            result[i, at_g, :] = value
            values.append(value)

        @pl.when(level == HANDED)
        def _():
            solved[g] = jnp.concatenate(values, axis=0).astype(BF16)
            hand_solved(g).start()

    def advance(g, carry):
        step(g)

        @pl.when(kept & (g >= SKEW))
        def _():
            close(g - SKEW)

        return carry

    lax.fori_loop(0, groups, advance, 0)

    @pl.when(kept)
    def _():
        def finish(g, carry):
            close(g)
            return carry

        lax.fori_loop(groups - SKEW, groups, finish, 0)

    @pl.when(jnp.logical_not(kept))
    def _():
        def returned(g, carry):
            wait_for(back.at[g], back_recv.at[g])
            return carry

        lax.fori_loop(jnp.where(level == 0, groups - WINDOW, 0), groups, returned, 0)
        for i in range(fronts):
            at = i * UNIT
            value = jnp.concatenate([back[g].astype(F32)[at : at + UNIT] for g in range(groups)], axis=0)
            result[i] = apply(value, flat(finv, i))

    ungroup = jnp.where(square_row == packed_place(square_col), 1.0, 0.0).astype(BF16)
    for i in range(fronts):
        value = dot(ungroup, result[i].astype(BF16)).astype(BF16)
        for t in range(doubled // LANES):
            out_ref[0, i, :, t * LANES : (t + 1) * LANES] = value[t * total_rows : (t + 1) * total_rows]

    @pl.when(jnp.logical_not(kept))
    def _():
        wait_for(told, told_sem)
        for i in range(fronts):
            hand_inverse(i).wait_send()

        def drain(g, carry):
            wait_for(sent.at[g], sent_sem.at[g])
            hand_field(g).wait_send()
            return carry

        lax.fori_loop(0, groups, drain, 0)

    @pl.when(fused)
    def _():
        def drain(g, carry):
            hand_back(g).wait_send()
            return carry

        lax.fori_loop(0, groups, drain, 0)

    @pl.when(kept)
    def _():
        def drain(g, carry):
            wait_for(others(sent.at[g]), sent_sem.at[g])
            return carry

        lax.fori_loop(0, groups, drain, 0)

    @pl.when(level == HANDED)
    def _():
        def drain(g, carry):
            hand_solved(g).wait_send()
            return carry

        lax.fori_loop(0, groups, drain, 0)


def body(leafs, sweeps, rhs, incoming, front_inv, coupling, update, dest_owner, dest_front):
    fronts, total_rows, doubled = incoming.shape
    width = doubled // 2
    blocks = dest_owner.shape[1]
    groups = total_rows // ROWS
    slots = leafs * PER
    pairs = fronts * blocks
    vmem = pl.BlockSpec(memory_space=pltpu.VMEM)
    hbm = pl.BlockSpec(memory_space=pl.ANY)
    dma = pltpu.SemaphoreType.DMA
    return pl.pallas_call(
        functools.partial(kernel, leafs, sweeps),
        out_shape=jax.ShapeDtypeStruct(rhs.shape, BF16),
        in_specs=[hbm, hbm, hbm, hbm, hbm, vmem, vmem],
        out_specs=vmem,
        scratch_shapes=[
            pltpu.VMEM(incoming.shape, BF16),
            pltpu.VMEM(incoming.shape, BF16),
            pltpu.VMEM(front_inv.shape[1:], BF16),
            pltpu.VMEM(coupling.shape[1:], BF16),
            pltpu.VMEM(update.shape[1:], BF16),
            pltpu.VMEM(front_inv.shape[1:], BF16),
            pltpu.VMEM((fronts, 2 * width, width), BF16),
            pltpu.VMEM((fronts, 2 * width, blocks * width), BF16),
            pltpu.VMEM((slots, pairs * UNIT), BF16),
            pltpu.VMEM((fronts * UNIT, slots), BF16),
            pltpu.VMEM((groups, fronts * UNIT, LANES), F32),
            pltpu.VMEM((groups, pairs * UNIT, LANES), F32),
            pltpu.VMEM((groups, fronts * UNIT, LANES), BF16),
            pltpu.VMEM((groups, fronts * UNIT, LANES), BF16),
            pltpu.VMEM((groups, fronts * UNIT, LANES), F32),
            pltpu.VMEM((fronts, groups * UNIT, LANES), F32),
            pltpu.VMEM((groups, fronts * UNIT, LANES), BF16),
            pltpu.VMEM((groups, fronts * UNIT, LANES), BF16),
            pltpu.VMEM((groups, slots, LANES), BF16),
            pltpu.VMEM((groups, slots, LANES), BF16),
            pltpu.VMEM((groups, slots, LANES), BF16),
            pltpu.VMEM((slots, LANES), BF16),
            pltpu.VMEM((slots, LANES), BF16),
            dma((5, fronts)),
            dma((fronts,)),
            dma((fronts,)),
            dma((groups,)),
            dma((groups,)),
            dma((groups,)),
            dma((groups,)),
            dma((groups,)),
            dma((groups,)),
            dma((groups,)),
            dma((groups,)),
            dma((groups,)),
            dma,
            dma,
        ],
        compiler_params=pltpu.CompilerParams(
            collective_id=0, has_side_effects=True, vmem_limit_bytes=60 * 1024 * 1024
        ),
    )(rhs[0], incoming, front_inv[0], coupling[0], update[0], dest_owner.T, dest_front.T)


def solution(mesh):
    return jax.shard_map(
        functools.partial(body, mesh.shape["leaf"], mesh.shape["sweep"]),
        mesh=mesh,
        in_specs=(
            P("sweep", "leaf", None, None),
            P("leaf", None, None),
            P("sweep", "leaf", None, None, None),
            P("sweep", "leaf", None, None, None),
            P("sweep", "leaf", None, None, None, None),
            P("leaf", None),
            P("leaf", None),
        ),
        out_specs=P("sweep", "leaf", None, None),
        check_vma=False,
    )
```

```python
import functools

import jax
import jax.numpy as jnp
from jax import lax
from jax.experimental import pallas as pl
from jax.experimental.pallas import tpu as pltpu
from jax.sharding import PartitionSpec as P

ROWS = 2
SLOTS = 2
LANES = 128
TOGETHER = 4
LEAF_X = 4
UNIT = 8
PER = SLOTS * UNIT
SKEW = 2
WINDOW = 4
HANDED = 1
MESH = pl.DeviceIdType.MESH
F32 = jnp.float32
BF16 = jnp.bfloat16


def dot(a, b):
    return jnp.dot(a, b, preferred_element_type=F32)


def expand(v):
    a = v.reshape(v.shape[0] // UNIT, UNIT, LANES)
    b = pltpu.roll(a, UNIT // 2, 1)
    row = lax.broadcasted_iota(jnp.int32, a.shape, 1)
    first = jnp.where(row < UNIT // 2, a, b)
    second = jnp.where(row < UNIT // 2, b, a)
    real = row % (UNIT // 2) < ROWS
    parts = [first, second]
    for half in (first, second):
        swapped = pltpu.roll(half, ROWS, 1)
        parts.append(jnp.where(real, -swapped, swapped))
    return jnp.concatenate(parts, axis=2).reshape(v.shape[0], 4 * LANES).astype(BF16)


def collapse(p):
    a = p.reshape(p.shape[0] // UNIT, UNIT, 2 * LANES)
    row = lax.broadcasted_iota(jnp.int32, (a.shape[0], UNIT, LANES), 1)
    return jnp.where(row < UNIT // 2, a[:, :, :LANES], a[:, :, LANES:]).reshape(p.shape[0], LANES)


def beside(m):
    half = m.shape[0] // 2
    return jnp.concatenate([m, jnp.concatenate([-m[half:], m[:half]], axis=0)], axis=1)


def kernel(
    leafs, sweeps, rhs_hbm, inc_hbm, finv_hbm, coup_hbm, upd_hbm, own_ref, front_ref, out_ref,
    rhs_ref, inc_ref, finv, coup, upd, above, comp_d, comp_u, place, take, rhs_s, rhs_u, rest, back, above_field,
    result, solved, entered, sent, got, last, told, heard,
    load_sem, above_send, above_recv, field_send, field_recv, back_send, back_recv, solved_send, entered_recv, sent_sem, got_sem, last_sem,
    told_sem, heard_sem,
):
    fronts, total_rows, doubled = inc_ref.shape
    width = doubled // 2
    blocks = own_ref.shape[0]
    groups = total_rows // ROWS
    pairs = fronts * blocks
    top = sweeps - 1
    me = lax.axis_index("leaf")
    level = lax.axis_index("sweep")
    kept = (level == HANDED) | (level == top)
    entry = level == HANDED + 1
    fused = (level > 0) & (level != HANDED + 1)

    def load(which, i):
        source, target = ((finv_hbm, finv), (coup_hbm, coup), (upd_hbm, upd), (rhs_hbm, rhs_ref), (inc_hbm, inc_ref))[which]
        return pltpu.make_async_copy(source.at[i], target.at[i], load_sem.at[which, i])

    for i in range(fronts):
        for which in (3, 4, 1, 0, 2):
            load(which, i).start()

    barrier = pltpu.get_barrier_semaphore()

    @pl.when(fused)
    def _():
        for to in range(leafs):
            pl.semaphore_signal(barrier, inc=1, device_id=(level - 1, to), device_id_type=MESH)

    @pl.when(entry)
    def _():
        pl.semaphore_signal(barrier, inc=1, device_id=(level - 1, me), device_id_type=MESH)

    @pl.when(jnp.logical_not(kept))
    def _():
        pl.semaphore_signal(barrier, inc=1, device_id=(level + 1, me), device_id_type=MESH)

    @pl.when(kept)
    def _():
        for off in range(1, leafs):
            pl.semaphore_signal(barrier, inc=1, device_id=(level, lax.rem(me + off, leafs)), device_id_type=MESH)

    lane = lax.broadcasted_iota(jnp.int32, (fronts, pairs * UNIT), 1)
    sub = lax.broadcasted_iota(jnp.int32, (fronts, pairs * UNIT), 0)
    lane_front = lane // (blocks * UNIT)
    lane_block = (lane // UNIT) % blocks
    own = own_ref[...].T
    front = front_ref[...].T
    own_l = jnp.zeros_like(lane)
    front_l = jnp.zeros_like(lane)
    for k in range(blocks):
        here = (lane_block == k) & (lane_front == sub)
        own_l += jnp.where(here, own[:, k : k + 1], 0)
        front_l += jnp.where(here, front[:, k : k + 1] + 1, 0)
    own_l = jnp.sum(own_l, axis=0, keepdims=True)
    front_l = jnp.sum(front_l, axis=0, keepdims=True)
    rank = jnp.zeros_like(lane)
    for k in range(blocks):
        rank += jnp.where((own[:, k : k + 1] == own_l) & (sub < lane_front), 1, 0)
    rank = jnp.sum(rank, axis=0, keepdims=True)
    goal = (own_l * SLOTS + rank) * UNIT + lane[:1] % UNIT
    row = lax.broadcasted_iota(jnp.int32, (leafs * PER, pairs * UNIT), 0)
    hot = row == goal
    place[...] = jnp.where(hot, 1.0, 0.0).astype(BF16)
    labels = jnp.where(hot, front_l.astype(F32), 0.0).astype(BF16)
    told[...] = dot(labels, jnp.ones((pairs * UNIT, LANES), BF16)).astype(BF16)

    waits = jnp.where(kept, leafs - 1, leafs) + jnp.where(fused, 1, 0) + jnp.where(level == HANDED, 1, 0)
    pl.semaphore_wait(barrier, waits)

    leaf_z = leafs // LEAF_X
    steps = [(dz, dx) for dz in range(leaf_z) for dx in range(LEAF_X)]
    steps.sort(key=lambda d: -min(d[0], leaf_z - d[0]) - min(d[1], LEAF_X - d[1]))

    mine = pl.ds(pl.multiple_of(me * PER, PER), PER)

    def spread(source, target, sends, recvs, to_level, offsets):
        for dz, dx in offsets:
            to = lax.rem(me // LEAF_X + dz, leaf_z) * LEAF_X + lax.rem(me % LEAF_X + dx, LEAF_X)
            pltpu.make_async_remote_copy(
                src_ref=source.at[pl.ds(pl.multiple_of(to * PER, PER), PER)],
                dst_ref=target.at[mine],
                send_sem=sends,
                recv_sem=recvs,
                device_id=(to_level, to),
                device_id_type=MESH,
            ).start()

    def wait_for(ref, sem):
        pltpu.make_async_copy(ref, ref, sem).wait()

    def others(ref):
        return ref.at[pl.ds(0, (leafs - 1) * PER)]

    def hand(source, target, send, recv, to_level):
        return pltpu.make_async_remote_copy(
            src_ref=source,
            dst_ref=target,
            send_sem=send,
            recv_sem=recv,
            device_id=(to_level, me),
            device_id_type=MESH,
        )

    def hand_inverse(i):
        return hand(finv_hbm.at[i], above.at[i], above_send.at[i], above_recv.at[i], level + 1)

    def hand_field(g):
        return hand(rhs_s.at[g], above_field.at[g], field_send.at[g], field_recv.at[g], level + 1)

    def hand_solved(g):
        return hand(solved.at[g], entered.at[g], solved_send.at[g], entered_recv.at[g], level + 1)

    def hand_back(g):
        return hand(rest.at[g], back.at[g], back_send.at[g], back_recv.at[g], level - 1)

    @pl.when(jnp.logical_not(kept))
    def _():
        for i in range(fronts):
            hand_inverse(i).start()
        spread(told, heard, told_sem, heard_sem, level + 1, steps)

    def packed_place(index):
        at = (index // ROWS) % 2 * 2 + (index // (2 * ROWS)) % 2
        return at * total_rows + (index // UNIT) * ROWS + index % ROWS

    spots = groups * UNIT
    square_row = lax.broadcasted_iota(jnp.int32, (spots, spots), 0)
    square_col = lax.broadcasted_iota(jnp.int32, (spots, spots), 1)

    def packed(value):
        regroup = jnp.where(square_col == packed_place(square_row), 1.0, 0.0).astype(BF16)
        parts = [value[:, t * LANES : (t + 1) * LANES] for t in range(doubled // LANES)]
        return dot(regroup, jnp.concatenate(parts, axis=0))

    def apply(v, m):
        return collapse(dot(expand(v), m))

    def flat(ref, *at):
        return ref[at].reshape(2 * width, width)

    def rounded(v):
        return v.astype(BF16).astype(F32)

    starts = jnp.where(level == 0, 1.0, 0.0).astype(F32)

    def begin(b, carry):
        these = [b * TOGETHER + n for n in range(TOGETHER)]
        for i in these:
            for which in range(5):
                load(which, i).wait()
        entering = [expand(packed(inc_ref[i])) for i in these]
        fields = [packed(rhs_ref[i]) for i in these]
        fields = [
            field - starts * collapse(dot(x, flat(coup, i))) for i, x, field in zip(these, entering, fields)
        ]
        firsts = [expand(rounded(apply(rounded(field), flat(finv, i)))) for i, field in zip(these, fields)]
        for i, field in zip(these, fields):
            at_i = pl.ds(pl.multiple_of(i * UNIT, UNIT), UNIT)
            for g in range(groups):
                rhs_s[g, at_i, :] = field[g * UNIT : (g + 1) * UNIT]
        for i, first in zip(these, firsts):
            for k in range(blocks):
                part = collapse(dot(first, flat(upd, i, k)))
                at_ik = pl.ds(pl.multiple_of((i * blocks + k) * UNIT, UNIT), UNIT)
                for g in range(groups):
                    rhs_u[g, at_ik, :] = part[g * UNIT : (g + 1) * UNIT]
        return carry

    lax.fori_loop(0, fronts // TOGETHER, begin, 0)

    def compose(b, carry):
        these = [b * TOGETHER + n for n in range(TOGETHER)]
        for i in these:
            @pl.when(fused)
            def _():
                wait_for(above.at[i], above_recv.at[i])

            @pl.when(entry)
            def _():
                unit_row = lax.broadcasted_iota(jnp.int32, (width, width), 0)
                unit_col = lax.broadcasted_iota(jnp.int32, (width, width), 1)
                above[i, 0] = jnp.where(unit_row == unit_col, 1.0, 0.0).astype(BF16)
                above[i, 1] = jnp.zeros((width, width), BF16)

        downs = [dot(beside(flat(above, i)), flat(coup, i)).astype(BF16) for i in these]
        for i, down in zip(these, downs):
            comp_d[i] = down
        firsts = [beside(dot(beside(down), flat(finv, i)).astype(BF16)) for i, down in zip(these, downs)]
        for k in range(blocks):
            for i, first in zip(these, firsts):
                comp_u[i, :, k * width : (k + 1) * width] = dot(first, flat(upd, i, k)).astype(BF16)
        return carry

    @pl.when(level > 0)
    def _():
        lax.fori_loop(0, fronts // TOGETHER, compose, 0)

    @pl.when(fused)
    def _():
        wait_for(heard, heard_sem)
        h = heard[...].astype(F32)
        t_row = lax.broadcasted_iota(jnp.int32, h.shape, 0)
        t_lane = lax.broadcasted_iota(jnp.int32, h.shape, 1)
        fits = (h == (t_lane // UNIT + 1).astype(F32)) & (t_row % UNIT == t_lane % UNIT)
        take[...] = jnp.where(fits, 1.0, 0.0).T.astype(BF16)[: fronts * UNIT]

    def step(g):
        @pl.when((level == 0) & (g >= WINDOW))
        def _():
            wait_for(back.at[g - WINDOW], back_recv.at[g - WINDOW])

        @pl.when(level == 0)
        def _():
            sent[g] = dot(place[...], rhs_u[g].astype(BF16)).astype(BF16)

        @pl.when(fused)
        def _():
            wait_for(above_field.at[g], field_recv.at[g])
            wait_for(got.at[g], got_sem.at[g])

        @pl.when(entry)
        def _():
            wait_for(entered.at[g], entered_recv.at[g])

        @pl.when(level > 0)
        def _():
            summed = (above_field[g] - dot(take[...], got[g])).astype(BF16).astype(F32)
            remainder = jnp.where(entry, entered[g].astype(F32), summed)
            rest[g] = remainder.astype(BF16)
            x = expand(remainder)
            values = []
            for i in range(fronts):
                wide = dot(x[i * UNIT : (i + 1) * UNIT], comp_u[i])
                for k in range(blocks):
                    at = (i * blocks + k) * UNIT
                    values.append(rhs_u[g, at : at + UNIT, :] - collapse(wide[:, k * width : (k + 1) * width]))
            contrib = jnp.concatenate(values, axis=0).astype(BF16)
            sent[g] = dot(place[...], contrib).astype(BF16)

        @pl.when(fused)
        def _():
            hand_back(g).start()

        @pl.when(jnp.logical_not(kept))
        def _():
            spread(sent.at[g], got.at[g], sent_sem.at[g], got_sem.at[g], level + 1, steps)

        @pl.when(kept)
        def _():
            spread(sent.at[g], last.at[g], sent_sem.at[g], last_sem.at[g], level, steps[:-1])
            last[g, mine, :] = sent[g, mine, :]

        @pl.when(level > 0)
        def _():
            x = expand(rest[g].astype(F32))
            for i in range(fronts):
                at = i * UNIT
                value = collapse(dot(x[at : at + UNIT], comp_d[i]))
                rhs_s[g, at : at + UNIT, :] = rhs_s[g, at : at + UNIT, :] - value

        @pl.when(jnp.logical_not(kept))
        def _():
            hand_field(g).start()

    def close(g):
        wait_for(others(last.at[g]), last_sem.at[g])
        value = (rhs_s[g] - dot(take[...], last[g])).astype(BF16)
        x = expand(value.astype(F32))
        at_g = pl.ds(pl.multiple_of(g * UNIT, UNIT), UNIT)
        values = []
        for i in range(fronts):
            value = collapse(dot(x[i * UNIT : (i + 1) * UNIT], flat(finv, i)))
            result[i, at_g, :] = value
            values.append(value)

        @pl.when(level == HANDED)
        def _():
            solved[g] = jnp.concatenate(values, axis=0).astype(BF16)
            hand_solved(g).start()

    def advance(g, carry):
        step(g)

        @pl.when(kept & (g >= SKEW))
        def _():
            close(g - SKEW)

        return carry

    lax.fori_loop(0, groups, advance, 0)

    @pl.when(kept)
    def _():
        def finish(g, carry):
            close(g)
            return carry

        lax.fori_loop(groups - SKEW, groups, finish, 0)

    @pl.when(jnp.logical_not(kept))
    def _():
        def returned(g, carry):
            wait_for(back.at[g], back_recv.at[g])
            return carry

        lax.fori_loop(jnp.where(level == 0, groups - WINDOW, 0), groups, returned, 0)
        for i in range(fronts):
            at = i * UNIT
            value = jnp.concatenate([back[g].astype(F32)[at : at + UNIT] for g in range(groups)], axis=0)
            result[i] = apply(value, flat(finv, i))

    ungroup = jnp.where(square_row == packed_place(square_col), 1.0, 0.0).astype(BF16)
    for i in range(fronts):
        value = dot(ungroup, result[i].astype(BF16)).astype(BF16)
        for t in range(doubled // LANES):
            out_ref[0, i, :, t * LANES : (t + 1) * LANES] = value[t * total_rows : (t + 1) * total_rows]

    @pl.when(jnp.logical_not(kept))
    def _():
        wait_for(told, told_sem)
        for i in range(fronts):
            hand_inverse(i).wait_send()

        def drain(g, carry):
            wait_for(sent.at[g], sent_sem.at[g])
            hand_field(g).wait_send()
            return carry

        lax.fori_loop(0, groups, drain, 0)

    @pl.when(fused)
    def _():
        def drain(g, carry):
            hand_back(g).wait_send()
            return carry

        lax.fori_loop(0, groups, drain, 0)

    @pl.when(kept)
    def _():
        def drain(g, carry):
            wait_for(others(sent.at[g]), sent_sem.at[g])
            return carry

        lax.fori_loop(0, groups, drain, 0)

    @pl.when(level == HANDED)
    def _():
        def drain(g, carry):
            hand_solved(g).wait_send()
            return carry

        lax.fori_loop(0, groups, drain, 0)


def body(leafs, sweeps, rhs, incoming, front_inv, coupling, update, dest_owner, dest_front):
    fronts, total_rows, doubled = incoming.shape
    width = doubled // 2
    blocks = dest_owner.shape[1]
    groups = total_rows // ROWS
    slots = leafs * PER
    pairs = fronts * blocks
    vmem = pl.BlockSpec(memory_space=pltpu.VMEM)
    hbm = pl.BlockSpec(memory_space=pl.ANY)
    dma = pltpu.SemaphoreType.DMA
    return pl.pallas_call(
        functools.partial(kernel, leafs, sweeps),
        out_shape=jax.ShapeDtypeStruct(rhs.shape, BF16),
        in_specs=[hbm, hbm, hbm, hbm, hbm, vmem, vmem],
        out_specs=vmem,
        scratch_shapes=[
            pltpu.VMEM(incoming.shape, BF16),
            pltpu.VMEM(incoming.shape, BF16),
            pltpu.VMEM(front_inv.shape[1:], BF16),
            pltpu.VMEM(coupling.shape[1:], BF16),
            pltpu.VMEM(update.shape[1:], BF16),
            pltpu.VMEM(front_inv.shape[1:], BF16),
            pltpu.VMEM((fronts, 2 * width, width), BF16),
            pltpu.VMEM((fronts, 2 * width, blocks * width), BF16),
            pltpu.VMEM((slots, pairs * UNIT), BF16),
            pltpu.VMEM((fronts * UNIT, slots), BF16),
            pltpu.VMEM((groups, fronts * UNIT, LANES), F32),
            pltpu.VMEM((groups, pairs * UNIT, LANES), F32),
            pltpu.VMEM((groups, fronts * UNIT, LANES), BF16),
            pltpu.VMEM((groups, fronts * UNIT, LANES), BF16),
            pltpu.VMEM((groups, fronts * UNIT, LANES), F32),
            pltpu.VMEM((fronts, groups * UNIT, LANES), F32),
            pltpu.VMEM((groups, fronts * UNIT, LANES), BF16),
            pltpu.VMEM((groups, fronts * UNIT, LANES), BF16),
            pltpu.VMEM((groups, slots, LANES), BF16),
            pltpu.VMEM((groups, slots, LANES), BF16),
            pltpu.VMEM((groups, slots, LANES), BF16),
            pltpu.VMEM((slots, LANES), BF16),
            pltpu.VMEM((slots, LANES), BF16),
            dma((5, fronts)),
            dma((fronts,)),
            dma((fronts,)),
            dma((groups,)),
            dma((groups,)),
            dma((groups,)),
            dma((groups,)),
            dma((groups,)),
            dma((groups,)),
            dma((groups,)),
            dma((groups,)),
            dma((groups,)),
            dma,
            dma,
        ],
        compiler_params=pltpu.CompilerParams(
            collective_id=0, has_side_effects=True, vmem_limit_bytes=60 * 1024 * 1024
        ),
    )(rhs[0], incoming, front_inv[0], coupling[0], update[0], dest_owner.T, dest_front.T)


def solution(mesh):
    return jax.shard_map(
        functools.partial(body, mesh.shape["leaf"], mesh.shape["sweep"]),
        mesh=mesh,
        in_specs=(
            P("sweep", "leaf", None, None),
            P("leaf", None, None),
            P("sweep", "leaf", None, None, None),
            P("sweep", "leaf", None, None, None),
            P("sweep", "leaf", None, None, None, None),
            P("leaf", None),
            P("leaf", None),
        ),
        out_specs=P("sweep", "leaf", None, None),
        check_vma=False,
    )
```
